128 devices in a mesh: inner: 4 (over x_lo, core), outer: 32 (over y, z, x_hi).
Axes of the slice: x: 4 (x_hi: 2, x_lo: 2; x = x_hi * 2 + x_lo), y: 4, z: 4, core: 2. Of those that a mesh axis runs over, the one named last changes fastest.
Arguments:
- query_rows: bfloat16 [32768, 6144], P(('inner', 'outer')), may hold values from -16 to 16
- key_rows: bfloat16 [32768, 1024], P(('inner', 'outer')), may hold values from -16 to 16
- value_rows: bfloat16 [32768, 1024], P(('inner', 'outer')), may hold values from -6 to 6
- out_grad: bfloat16 [32768, 6144], P(('inner', 'outer')), may hold values from -6 to 6
- doc_lengths: int32 [64], replicated, may hold values from 1 to 1025, 32768 in all
Outputs:
- attn_out: bfloat16 [32768, 6144], P(('inner', 'outer'))
- grad_query: bfloat16 [32768, 6144], P(('inner', 'outer'))
- grad_key: bfloat16 [32768, 1024], P(('inner', 'outer'))
- grad_value: bfloat16 [32768, 1024], P(('inner', 'outer'))
The draws below stay inside these ranges and needn't reach their ends.
Inputs may be any that keep to these rules, and one draw needn't show every extreme that they name: `doc_lengths`: the lengths, in order, of the 64 documents packed into the sequence; they sum to 32768.
All inputs are finite; a program needn't handle non-finite values.
Results may differ from the reference program's by a relative error of at most 0.014.
Values may be sent and summed in bfloat16 or wider, within the bound.
No kernel may reach another device: no remote copies, remote signals or barrier semaphores. Data moves between devices by JAX's collectives and lax.ppermute only.
A program may use at most 192 MiB of HBM per device.

```python
import math
import jax
import jax.numpy as jnp
import numpy as np
from jax import lax

KVH = 8
GROUP = 6
DH = 128
TOK_DEV = 256
REACH = 4
TOKENS = 32768
MOST = 1025
DOCS = 64


def draw_query_rows(key, part):
    key = jax.random.fold_in(key, 1)
    drawn = jax.random.truncated_normal(key, -3.5, 3.5, (TOKENS, KVH * GROUP * DH), jnp.float32)
    return drawn.astype(jnp.bfloat16)


def draw_key_rows(key, part):
    key = jax.random.fold_in(key, 7)
    drawn = jax.random.truncated_normal(key, -3.5, 3.5, (TOKENS, KVH * DH), jnp.float32)
    return drawn.astype(jnp.bfloat16)


def block_levels(key, extent, cuts, low, largest):
    level = 1.0
    for position, shards_of in cuts:
        draws = jax.random.uniform(jax.random.fold_in(jax.random.fold_in(key, 6), position), (shards_of,), jnp.float32, low / len(cuts), largest / len(cuts))
        level = level * jnp.repeat(jnp.exp(draws), extent[position] // shards_of).reshape((-1,) + (1,) * (len(extent) - 1 - position))
    return level


def profile(count, total, bound, slope):
    portions = [(1 << 20) // math.isqrt(standing ** slope) + 1 for standing in range(2, count + 1)]
    surplus, holding = total - bound - (count - 1), [1] * (count - 1)
    while surplus > 0:
        movable = [i for i in range(count - 1) if holding[i] < bound]
        whole, remaining = sum([portions[i] for i in movable]), surplus
        for i in movable:
            addition = min(bound - holding[i], max(1, remaining * portions[i] // whole), surplus)
            holding[i] = holding[i] + addition
            surplus = surplus - addition
    return np.array([bound] + holding)


def uneven_parts(own_key, number_of, total, most, lean):
    if number_of == 2:
        one = jax.random.randint(own_key, (), max(1, total - most), min(most, total - 1) + 1)
        return jnp.stack([one, total - one])
    sizes = jnp.asarray(profile(number_of, total, most, lean), jnp.int32)
    twos = (number_of - 1) // 2
    source_of, taker = sizes[1:1 + 2 * twos:2], sizes[2:2 + 2 * twos:2]
    room = jnp.minimum(source_of - 1, most - taker)
    moved = jax.random.randint(jax.random.fold_in(own_key, 1), (twos,), 0, 1 << 20) % (room + 1)
    sizes = sizes.at[1:1 + 2 * twos:2].set(source_of - moved).at[2:2 + 2 * twos:2].set(taker + moved)
    return sizes[jax.random.permutation(jax.random.fold_in(own_key, 2), number_of)]


def bell_draw(key, extent, scale, bound, split=(), kind=jnp.bfloat16):
    level = block_levels(key, extent, split, -0.22, 0.18) if split else 1.0
    result = jax.random.normal(key, extent, jnp.float32) * scale * level
    return jnp.minimum(jnp.maximum(result, -bound), bound).astype(kind)


def setup_inputs(seed: int = 0) -> dict:
    splits = jax.random.split(jax.random.key(seed), 6)
    return {
        "query_rows": draw_query_rows(jax.random.fold_in(splits[5], 71), 0),
        "key_rows": draw_key_rows(jax.random.fold_in(splits[5], 71), 0),
        "value_rows": bell_draw(splits[2], (TOKENS, KVH * DH), 1.0, 6.0, ((0, 128),)),
        "out_grad": bell_draw(splits[3], (TOKENS, KVH * GROUP * DH), 1.0, 6.0, ((0, 128),)),
        "doc_lengths": uneven_parts(splits[4], DOCS, TOKENS, MOST, 2).astype(jnp.int32),
    }


def document_of(doc_lengths, positions):
    boundaries = jnp.cumsum(doc_lengths, dtype=jnp.int32)
    hits = (boundaries[None, :] <= positions[:, None]).astype(jnp.int32)
    return jnp.sum(hits, axis=1, dtype=jnp.int32)


def attend_block(query_block, grad_block, key_window, value_window, allowed):
    score_scale = DH ** -0.5
    query_f = query_block.astype(jnp.float32)
    grad_f = grad_block.astype(jnp.float32)
    key_f = key_window.astype(jnp.float32)
    value_f = value_window.astype(jnp.float32)
    scores = jnp.einsum("tkgd,wkd->kgtw", query_f, key_f) * score_scale
    scores = jnp.where(allowed[None, None], scores, -jnp.inf)
    row_peak = jnp.max(scores, axis=3, keepdims=True)
    exp_scores = jnp.exp(scores - row_peak)
    probs = exp_scores / jnp.sum(exp_scores, axis=3, keepdims=True)
    weights = probs.astype(jnp.bfloat16)
    weights_f = weights.astype(jnp.float32)
    attn_block = jnp.einsum("kgtw,wkd->tkgd", weights_f, value_f).astype(jnp.bfloat16)
    dweights = jnp.einsum("tkgd,wkd->kgtw", grad_f, value_f)
    row_delta = jnp.sum(probs * dweights, axis=3, keepdims=True)
    dscores = (probs * (dweights - row_delta) * score_scale).astype(jnp.bfloat16)
    dscores_f = dscores.astype(jnp.float32)
    dquery = jnp.einsum("kgtw,wkd->tkgd", dscores_f, key_f).astype(jnp.bfloat16)
    dkey = jnp.einsum("kgtw,tkgd->wkd", dscores_f, query_f)
    dvalue = jnp.einsum("kgtw,tkgd->wkd", weights_f, grad_f)
    dkey = lax.optimization_barrier(dkey.astype(jnp.bfloat16)).astype(jnp.float32)
    dvalue = lax.optimization_barrier(dvalue.astype(jnp.bfloat16)).astype(jnp.float32)
    return attn_block, dquery, dkey, dvalue


def reference(query_rows, key_rows, value_rows, out_grad, doc_lengths):
    reach_rows = REACH * TOK_DEV
    window_rows = reach_rows + TOK_DEV
    block_count = TOKENS // TOK_DEV
    key_padded = jnp.concatenate([jnp.zeros((reach_rows, KVH * DH), key_rows.dtype), key_rows], axis=0)
    value_padded = jnp.concatenate([jnp.zeros((reach_rows, KVH * DH), value_rows.dtype), value_rows], axis=0)

    def step(carried, block_index):
        dkey_total, dvalue_total = carried
        start = block_index * TOK_DEV
        query_block = lax.dynamic_slice_in_dim(query_rows, start, TOK_DEV, 0).reshape(TOK_DEV, KVH, GROUP, DH)
        grad_block = lax.dynamic_slice_in_dim(out_grad, start, TOK_DEV, 0).reshape(TOK_DEV, KVH, GROUP, DH)
        key_window = lax.dynamic_slice_in_dim(key_padded, start, window_rows, 0).reshape(window_rows, KVH, DH)
        value_window = lax.dynamic_slice_in_dim(value_padded, start, window_rows, 0).reshape(window_rows, KVH, DH)
        query_pos = start + jnp.arange(TOK_DEV, dtype=jnp.int32)
        key_pos = start - reach_rows + jnp.arange(window_rows, dtype=jnp.int32)
        same_doc = document_of(doc_lengths, query_pos)[:, None] == document_of(doc_lengths, key_pos)[None, :]
        allowed = same_doc & (key_pos[None, :] <= query_pos[:, None]) & (key_pos[None, :] >= 0)
        attn_block, dquery, dkey, dvalue = attend_block(query_block, grad_block, key_window, value_window, allowed)
        old_key = lax.dynamic_slice_in_dim(dkey_total, start, window_rows, 0)
        dkey_total = lax.dynamic_update_slice_in_dim(dkey_total, old_key + dkey.reshape(window_rows, KVH * DH), start, 0)
        old_value = lax.dynamic_slice_in_dim(dvalue_total, start, window_rows, 0)
        dvalue_total = lax.dynamic_update_slice_in_dim(dvalue_total, old_value + dvalue.reshape(window_rows, KVH * DH), start, 0)
        return (dkey_total, dvalue_total), (attn_block.reshape(TOK_DEV, KVH * GROUP * DH), dquery.reshape(TOK_DEV, KVH * GROUP * DH))

    start_totals = (jnp.zeros((TOKENS + reach_rows, KVH * DH), jnp.float32), jnp.zeros((TOKENS + reach_rows, KVH * DH), jnp.float32))
    totals, stacked = lax.scan(step, start_totals, jnp.arange(block_count, dtype=jnp.int32))
    attn_out = stacked[0].reshape(TOKENS, KVH * GROUP * DH)
    grad_query = stacked[1].reshape(TOKENS, KVH * GROUP * DH)
    grad_key = totals[0][reach_rows:].astype(jnp.bfloat16)
    grad_value = totals[1][reach_rows:].astype(jnp.bfloat16)
    return (attn_out, grad_query, grad_key, grad_value)
```

```python
import functools

import jax
import jax.numpy as jnp
from jax import lax
from jax.experimental import pallas as pl
from jax.experimental.pallas import tpu as pltpu
from jax.sharding import PartitionSpec as P

KVH = 8
GROUP = 6
DH = 128
REACH = 4
SLOTS = REACH + 1
TOK = 256
AXES = ("inner", "outer")
SCALE = DH ** (-0.5)
LOG2E = 1.4426950408889634
MASKED = -1e30
CHUNKS = 2
NN = (((1,), (0,)), ((), ()))
NT = (((1,), (1,)), ((), ()))


def mm(left, right, dims=NN):
    return lax.dot_general(left, right, dims, preferred_element_type=jnp.float32)


def attention_body(aliased, lo_ref, q_ref, g_ref, *refs):
    kv = refs[:SLOTS]
    refs = refs[SLOTS + aliased :]
    out_ref, dq_ref = refs[:2]
    dkv = refs[2 : 2 + SLOTS]
    bias_ref, t_ref, w_ref, ds_ref = refs[2 + SLOTS :]

    @pl.when(pl.program_id(0) == 0)
    def _():
        lo = lo_ref[...]
        qpos = lax.broadcasted_iota(jnp.int32, (TOK, TOK), 1)
        kpos = lax.broadcasted_iota(jnp.int32, (TOK, TOK), 0)
        for d in range(SLOTS):
            k = kpos - d * TOK
            ok = (k >= lo) & (k <= qpos)
            bias_ref[d] = jnp.where(ok, 0.0, MASKED)

    for h in range(GROUP):
        cols = slice(h * DH, (h + 1) * DH)
        qc = slice(h * TOK, (h + 1) * TOK)
        q = q_ref[:, cols]
        g = g_ref[:, cols]
        peak = None
        for d in range(SLOTS):
            t = mm(kv[d][0], q, NT) * (SCALE * LOG2E) + bias_ref[d]
            t_ref[d] = t
            part = jnp.max(t, axis=0, keepdims=True)
            peak = part if peak is None else jnp.maximum(peak, part)
        total = None
        for d in range(SLOTS):
            e = jnp.exp2(t_ref[d] - peak)
            t_ref[d] = e
            part = jnp.sum(e, axis=0, keepdims=True)
            total = part if total is None else total + part
        inverse = 1.0 / total
        out = None
        for d in range(SLOTS):
            p = t_ref[d] * inverse
            t_ref[d] = p
            w = p.astype(jnp.bfloat16)
            w_ref[d, :, qc] = w
            part = mm(kv[d][1].T, w)
            out = part if out is None else out + part
        out_ref[:, cols] = out.T.astype(jnp.bfloat16)
        delta = jnp.sum(out * g.astype(jnp.float32).T, axis=0, keepdims=True)
        dq = None
        for d in range(SLOTS):
            dp = mm(kv[d][1], g, NT)
            s = (t_ref[d] * (dp - delta)).astype(jnp.bfloat16)
            ds_ref[d, :, qc] = s
            part = mm(kv[d][0].T, s)
            dq = part if dq is None else dq + part
        dq_ref[:, cols] = (dq * SCALE).T.astype(jnp.bfloat16)
    qs = jnp.concatenate([q_ref[:, h * DH : (h + 1) * DH] for h in range(GROUP)], axis=0)
    gs = jnp.concatenate([g_ref[:, h * DH : (h + 1) * DH] for h in range(GROUP)], axis=0)
    for d in range(SLOTS):
        dkv[d][0] = (mm(ds_ref[d], qs) * SCALE).astype(jnp.bfloat16)
        dkv[d][1] = mm(w_ref[d], gs).astype(jnp.bfloat16)


def attend(lo, query_rows, out_grad, kvs, first, heads, earlier):
    big = pl.BlockSpec((TOK, GROUP * DH), lambda i: (0, first + i))
    small = pl.BlockSpec((2, TOK, DH), lambda i: (0, 0, i))
    aliased = len(earlier)
    big_shape = jax.ShapeDtypeStruct(query_rows.shape, jnp.bfloat16)
    small_shape = jax.ShapeDtypeStruct((2, TOK, heads * DH), jnp.bfloat16)
    window = SLOTS * TOK
    pairs = heads * GROUP * TOK * window
    return pl.pallas_call(
        functools.partial(attention_body, aliased),
        grid=(heads,),
        in_specs=[pl.BlockSpec((1, TOK), lambda i: (0, 0)), big, big]
        + [small] * SLOTS
        + [pl.BlockSpec(memory_space=pl.ANY)] * aliased,
        out_specs=[big, big] + [small] * SLOTS,
        out_shape=[big_shape, big_shape] + [small_shape] * SLOTS,
        scratch_shapes=[
            pltpu.VMEM((SLOTS, TOK, TOK), jnp.float32),
            pltpu.VMEM((SLOTS, TOK, TOK), jnp.float32),
            pltpu.VMEM((SLOTS, TOK, GROUP * TOK), jnp.bfloat16),
            pltpu.VMEM((SLOTS, TOK, GROUP * TOK), jnp.bfloat16),
        ],
        input_output_aliases={3 + SLOTS + n: n for n in range(aliased)},
        cost_estimate=pl.CostEstimate(
            flops=24 * pairs * DH,
            bytes_accessed=heads * TOK * DH * 2 * (4 * GROUP + 4 * SLOTS),
            transcendentals=pairs,
        ),
        compiler_params=pltpu.CompilerParams(vmem_limit_bytes=48 * 2**20),
    )(lo, query_rows, out_grad, *kvs, *earlier)


def moved(value, steps, count):
    return lax.ppermute(
        value, AXES, [(i, i + steps) for i in range(count) if 0 <= i + steps < count]
    )


def swapped(value, count):
    return lax.ppermute(value, AXES, [(i, i ^ 1) for i in range(count)])


def on_device(query_rows, key_rows, value_rows, out_grad, doc_lengths):
    count = lax.axis_size(AXES)
    me = lax.axis_index(AXES)
    even = (me % 2) == 0
    ends = jnp.cumsum(doc_lengths, dtype=jnp.int32)
    position = me * TOK + jnp.arange(TOK, dtype=jnp.int32)
    starts = jnp.max(jnp.where(ends[:, None] <= position[None, :], ends[:, None], 0), axis=0)
    lo = (starts - me * TOK)[None, :]
    heads = KVH // CHUNKS
    width = heads * DH
    windows = []
    for c in range(CHUNKS):
        cols = slice(c * width, (c + 1) * width)
        own = jnp.stack([key_rows[:, cols], value_rows[:, cols]])
        two = moved(own, 2, count)
        four = moved(two, 2, count)
        one = swapped(jnp.where(even, own, two), count)
        three = swapped(jnp.where(even, two, four), count)
        windows.append([own, one, two, three, four])
    earlier = []
    grads = []
    for c in range(CHUNKS):
        got = attend(lo, query_rows, out_grad, windows[c], c * heads, heads, earlier)
        earlier = list(got[:2])
        p0, p1, p2, p3, p4 = got[2:]
        f32 = jnp.float32
        y3 = swapped(p3, count).astype(f32)
        y1 = swapped(p1, count).astype(f32)
        zero = jnp.zeros_like(y1)
        s4 = (p4.astype(f32) + jnp.where(even, zero, y3)).astype(jnp.bfloat16)
        z4 = moved(s4, -2, count).astype(f32)
        s2 = (p2.astype(f32) + jnp.where(even, y3, y1) + z4).astype(jnp.bfloat16)
        z2 = moved(s2, -2, count).astype(f32)
        total = p0.astype(f32) + jnp.where(even, y1, zero) + z2
        grads.append(total.astype(jnp.bfloat16))
    grad_key = jnp.concatenate([part[0] for part in grads], axis=1)
    grad_value = jnp.concatenate([part[1] for part in grads], axis=1)
    return (earlier[0], earlier[1], grad_key, grad_value)


def solution(mesh):
    rows = P(AXES, None)
    return jax.shard_map(
        on_device,
        mesh=mesh,
        in_specs=(rows, rows, rows, rows, P()),
        out_specs=(rows, rows, rows, rows),
        check_vma=False,
    )
```

```python
import functools

import jax
import jax.numpy as jnp
from jax import lax
from jax.experimental import pallas as pl
from jax.experimental.pallas import tpu as pltpu
from jax.sharding import PartitionSpec as P

KVH = 8
GROUP = 6
DH = 128
REACH = 4
SLOTS = REACH + 1
TOK = 256
AXES = ("inner", "outer")
SCALE = DH ** (-0.5)
LOG2E = 1.4426950408889634
MASKED = -1e30
WIDE = 3
SPLIT = 2
PRE = False
TIE = True
NN = (((1,), (0,)), ((), ()))
NT = (((1,), (1,)), ((), ()))


def mm(left, right, dims=NN):
    return lax.dot_general(left, right, dims, preferred_element_type=jnp.float32)


def attention_body(aliased, lo_ref, q_ref, g_ref, *refs):
    kv = refs[:SLOTS]
    refs = refs[SLOTS + aliased :]
    out_ref, dq_ref = refs[:2]
    dkv = refs[2 : 2 + SLOTS]
    bias_ref, e_refs, w_ref, ds_ref, kt_ref, vt_ref, qt_ref, gt_ref = refs[2 + SLOTS :]

    @pl.when(pl.program_id(0) == 0)
    def _():
        lo = lo_ref[...]
        qpos = lax.broadcasted_iota(jnp.int32, (TOK, TOK), 1)
        kpos = lax.broadcasted_iota(jnp.int32, (TOK, TOK), 0)
        for d in range(SLOTS):
            k = kpos - d * TOK
            ok = (k >= lo) & (k <= qpos)
            bias_ref[d * TOK : (d + 1) * TOK] = jnp.where(ok, 0.0, MASKED)

    for d in range(SLOTS):
        rows = slice(d * TOK, (d + 1) * TOK)
        kt_ref[:, rows] = kv[d][0].T
        vt_ref[:, rows] = kv[d][1].T
    for h in range(GROUP):
        cols = slice(h * DH, (h + 1) * DH)
        qc = slice(h * TOK, (h + 1) * TOK)
        qt_ref[:, qc] = q_ref[:, cols].T
        gt_ref[:, qc] = g_ref[:, cols].T
    for first in range(0, GROUP, WIDE):
        wide = slice(first * TOK, (first + WIDE) * TOK)
        for h in range(first, first + WIDE):
            e_ref = e_refs.at[h % 2]
            qc = slice(h * TOK, (h + 1) * TOK)
            qt = qt_ref[:, qc]
            peaks, sums = [], []
            for d in range(SLOTS):
                rows = slice(d * TOK, (d + 1) * TOK)
                t = mm(kv[d][0], qt) * (SCALE * LOG2E) + bias_ref[rows]
                peak = jnp.max(t, axis=0, keepdims=True)
                e = jnp.exp2(t - peak)
                sums.append(jnp.sum(e, axis=0, keepdims=True))
                peaks.append(peak)
                e_ref[rows] = e
            top = functools.reduce(jnp.maximum, peaks)
            factors = [jnp.exp2(peak - top) for peak in peaks]
            inverse = 1.0 / functools.reduce(
                jnp.add, [part * factor for part, factor in zip(sums, factors)]
            )
            for d, factor in enumerate(factors):
                rows = slice(d * TOK, (d + 1) * TOK)
                w_ref[rows, qc] = (e_ref[rows] * (factor * inverse)).astype(jnp.bfloat16)
        out_wide = mm(vt_ref[...], w_ref[:, wide])
        for h in range(first, first + WIDE):
            cols = slice(h * DH, (h + 1) * DH)
            qc = slice(h * TOK, (h + 1) * TOK)
            gt = gt_ref[:, qc]
            out = out_wide[:, (h - first) * TOK : (h - first + 1) * TOK]
            out_ref[:, cols] = out.T.astype(jnp.bfloat16)
            delta = jnp.sum(out * gt.astype(jnp.float32), axis=0, keepdims=True)
            for d in range(SLOTS):
                rows = slice(d * TOK, (d + 1) * TOK)
                dp = mm(kv[d][1], gt)
                weights = w_ref[rows, qc].astype(jnp.float32)
                ds_ref[rows, qc] = (weights * (dp - delta)).astype(jnp.bfloat16)
        dq_wide = mm(kt_ref[...], ds_ref[:, wide]) * SCALE
        for n in range(WIDE):
            cols = slice((first + n) * DH, (first + n + 1) * DH)
            dq_ref[:, cols] = dq_wide[:, n * TOK : (n + 1) * TOK].T.astype(jnp.bfloat16)
    qs = jnp.concatenate([q_ref[:, h * DH : (h + 1) * DH] for h in range(GROUP)], axis=0)
    gs = jnp.concatenate([g_ref[:, h * DH : (h + 1) * DH] for h in range(GROUP)], axis=0)
    for d in range(SLOTS):
        rows = slice(d * TOK, (d + 1) * TOK)
        dkv[d][0] = (mm(ds_ref[rows], qs) * SCALE).astype(jnp.bfloat16)
        dkv[d][1] = mm(w_ref[rows], gs).astype(jnp.bfloat16)


def attend(lo, query_rows, out_grad, kvs, first, skip, heads, earlier):
    big = pl.BlockSpec((TOK, GROUP * DH), lambda i: (0, first + i))
    small = pl.BlockSpec((2, TOK, DH), lambda i: (0, 0, skip + i))
    part = pl.BlockSpec((2, TOK, DH), lambda i: (0, 0, i))
    aliased = len(earlier)
    big_shape = jax.ShapeDtypeStruct(query_rows.shape, jnp.bfloat16)
    small_shape = jax.ShapeDtypeStruct((2, TOK, heads * DH), jnp.bfloat16)
    window = SLOTS * TOK
    pairs = heads * GROUP * TOK * window
    return pl.pallas_call(
        functools.partial(attention_body, aliased),
        grid=(heads,),
        in_specs=[pl.BlockSpec((1, TOK), lambda i: (0, 0)), big, big]
        + [small] * SLOTS
        + [pl.BlockSpec(memory_space=pl.ANY)] * aliased,
        out_specs=[big, big] + [part] * SLOTS,
        out_shape=[big_shape, big_shape] + [small_shape] * SLOTS,
        scratch_shapes=[
            pltpu.VMEM((window, TOK), jnp.float32),
            pltpu.VMEM((2, window, TOK), jnp.float32),
            pltpu.VMEM((window, GROUP * TOK), jnp.bfloat16),
            pltpu.VMEM((window, GROUP * TOK), jnp.bfloat16),
            pltpu.VMEM((DH, window), jnp.bfloat16),
            pltpu.VMEM((DH, window), jnp.bfloat16),
            pltpu.VMEM((DH, GROUP * TOK), jnp.bfloat16),
            pltpu.VMEM((DH, GROUP * TOK), jnp.bfloat16),
        ],
        input_output_aliases={3 + SLOTS + n: n for n in range(aliased)},
        cost_estimate=pl.CostEstimate(
            flops=24 * pairs * DH,
            bytes_accessed=heads * TOK * DH * 2 * (4 * GROUP + 4 * SLOTS),
            transcendentals=pairs,
        ),
        compiler_params=pltpu.CompilerParams(vmem_limit_bytes=48 * 2**20),
    )(lo, query_rows, out_grad, *kvs, *earlier)


def moved(value, steps, count):
    return lax.ppermute(
        value, AXES, [(i, i + steps) for i in range(count) if 0 <= i + steps < count]
    )


def swapped(value, count):
    return lax.ppermute(value, AXES, [(i, i ^ 1) for i in range(count)])


def after(value, *earlier):
    return lax.optimization_barrier((value, *earlier))[0]


def on_device(query_rows, key_rows, value_rows, out_grad, doc_lengths):
    count = lax.axis_size(AXES)
    me = lax.axis_index(AXES)
    even = (me % 2) == 0
    ends = jnp.cumsum(doc_lengths, dtype=jnp.int32)
    position = me * TOK + jnp.arange(TOK, dtype=jnp.int32)
    starts = jnp.max(jnp.where(ends[:, None] <= position[None, :], ends[:, None], 0), axis=0)
    lo = (starts - me * TOK)[None, :]
    f32, bf16 = jnp.float32, jnp.bfloat16
    half = KVH // 2
    width = half * DH
    own0 = jnp.stack([key_rows[:, :width], value_rows[:, :width]])
    own1 = jnp.stack([key_rows[:, width:], value_rows[:, width:]])

    def call(window, chunk, skip, heads, earlier):
        got = attend(
            lo, query_rows, out_grad, window, chunk * half + skip, skip, heads, earlier
        )
        return list(got[:2]), got[2:]

    two0 = moved(own0, 2, count)
    one0 = swapped(jnp.where(even, own0, two0), count)
    four0 = moved(two0, 2, count)
    three0 = swapped(jnp.where(even, two0, four0), count)
    two1 = moved(after(own1, two0), 2, count)
    window = [own0, one0, two0, three0, four0]
    if PRE:
        three0, two1 = lax.optimization_barrier((three0, two1))
        window[3] = three0
    sendable = after(two1, three0)
    four1 = moved(sendable, 2, count)
    one1 = swapped(jnp.where(even, own1, sendable), count)
    big, a = call(window, 0, 0, SPLIT, [])
    three1 = swapped(jnp.where(even, two1, four1), count)
    if TIE:
        tied = lax.optimization_barrier((big, four1, one1))
        big, four1, one1 = tied
    big, b = call(window, 0, SPLIT, half - SPLIT, big)
    p0, p1, p2, p3, p4 = [jnp.concatenate(pair, axis=2) for pair in zip(a, b)]
    y3 = swapped(p3, count)
    window = [own1, one1, two1, three1, four1]
    big, a = call(window, 1, 0, SPLIT, big)
    if TIE:
        big, y3 = lax.optimization_barrier((big, y3))
    y1 = swapped(after(p1, y3), count).astype(f32)
    y3 = y3.astype(f32)
    s4 = (p4.astype(f32) + jnp.where(even, 0.0, y3)).astype(bf16)
    z4 = moved(s4, -2, count).astype(f32)
    big, b = call(window, 1, SPLIT, half - SPLIT, big)
    s2 = (p2.astype(f32) + jnp.where(even, y3, y1) + z4).astype(bf16)
    q0, q1, q2, q3, q4 = [jnp.concatenate(pair, axis=2) for pair in zip(a, b)]
    x3 = swapped(q3, count)
    z2 = moved(after(s2, big[0]), -2, count).astype(f32)
    total0 = p0.astype(f32) + jnp.where(even, y1, 0.0) + z2
    x1 = swapped(after(q1, x3), count).astype(f32)
    x3 = x3.astype(f32)
    s4 = (q4.astype(f32) + jnp.where(even, 0.0, x3)).astype(bf16)
    z4 = moved(s4, -2, count).astype(f32)
    s2 = (q2.astype(f32) + jnp.where(even, x3, x1) + z4).astype(bf16)
    z2 = moved(s2, -2, count).astype(f32)
    total1 = q0.astype(f32) + jnp.where(even, x1, 0.0) + z2
    grads = jnp.concatenate([total0.astype(bf16), total1.astype(bf16)], axis=2)
    return (big[0], big[1], grads[0], grads[1])


def solution(mesh):
    rows = P(AXES, None)
    return jax.shard_map(
        on_device,
        mesh=mesh,
        in_specs=(rows, rows, rows, rows, P()),
        out_specs=(rows, rows, rows, rows),
        check_vma=False,
    )
```

```python
import functools

import jax
import jax.numpy as jnp
from jax import lax
from jax.experimental import pallas as pl
from jax.experimental.pallas import tpu as pltpu
from jax.sharding import PartitionSpec as P

KVH = 8
GROUP = 6
DH = 128
REACH = 4
SLOTS = REACH + 1
TOK = 256
AXES = ("inner", "outer")
SCALE = DH ** (-0.5)
LOG2E = 1.4426950408889634
MASKED = -1e30
WIDE = 6
SPLIT = 2
PRE = False
TIE = True
NN = (((1,), (0,)), ((), ()))
NT = (((1,), (1,)), ((), ()))


def mm(left, right, dims=NN):
    return lax.dot_general(left, right, dims, preferred_element_type=jnp.float32)


def attention_body(aliased, lo_ref, q_ref, g_ref, *refs):
    kv = refs[:SLOTS]
    refs = refs[SLOTS + aliased :]
    out_ref, dq_ref = refs[:2]
    dkv = refs[2 : 2 + SLOTS]
    bias_ref, e_refs, w_ref, ds_ref, kt_ref, vt_ref, qt_ref, gt_ref = refs[2 + SLOTS :]

    @pl.when(pl.program_id(0) == 0)
    def _():
        lo = lo_ref[...]
        qpos = lax.broadcasted_iota(jnp.int32, (TOK, TOK), 1)
        kpos = lax.broadcasted_iota(jnp.int32, (TOK, TOK), 0)
        for d in range(SLOTS):
            k = kpos - d * TOK
            ok = (k >= lo) & (k <= qpos)
            bias_ref[d * TOK : (d + 1) * TOK] = jnp.where(ok, 0.0, MASKED)

    for d in range(SLOTS):
        rows = slice(d * TOK, (d + 1) * TOK)
        kt_ref[:, rows] = kv[d][0].T
        vt_ref[:, rows] = kv[d][1].T
    for h in range(GROUP):
        cols = slice(h * DH, (h + 1) * DH)
        qc = slice(h * TOK, (h + 1) * TOK)
        qt_ref[:, qc] = q_ref[:, cols].T
        gt_ref[:, qc] = g_ref[:, cols].T
    for first in range(0, GROUP, WIDE):
        wide = slice(first * TOK, (first + WIDE) * TOK)
        for h in range(first, first + WIDE):
            e_ref = e_refs.at[h % 2]
            qc = slice(h * TOK, (h + 1) * TOK)
            qt = qt_ref[:, qc]
            peaks, sums = [], []
            for d in range(SLOTS):
                rows = slice(d * TOK, (d + 1) * TOK)
                t = mm(kv[d][0], qt) * (SCALE * LOG2E) + bias_ref[rows]
                peak = jnp.max(t, axis=0, keepdims=True)
                e = jnp.exp2(t - peak)
                sums.append(jnp.sum(e, axis=0, keepdims=True))
                peaks.append(peak)
                e_ref[rows] = e
            top = functools.reduce(jnp.maximum, peaks)
            factors = [jnp.exp2(peak - top) for peak in peaks]
            inverse = 1.0 / functools.reduce(
                jnp.add, [part * factor for part, factor in zip(sums, factors)]
            )
            for d, factor in enumerate(factors):
                rows = slice(d * TOK, (d + 1) * TOK)
                w_ref[rows, qc] = (e_ref[rows] * (factor * inverse)).astype(jnp.bfloat16)
        out_wide = mm(vt_ref[...], w_ref[:, wide])
        for h in range(first, first + WIDE):
            cols = slice(h * DH, (h + 1) * DH)
            qc = slice(h * TOK, (h + 1) * TOK)
            gt = gt_ref[:, qc]
            out = out_wide[:, (h - first) * TOK : (h - first + 1) * TOK]
            out_ref[:, cols] = out.T.astype(jnp.bfloat16)
            delta = jnp.sum(out * gt.astype(jnp.float32), axis=0, keepdims=True)
            for d in range(SLOTS):
                rows = slice(d * TOK, (d + 1) * TOK)
                dp = mm(kv[d][1], gt)
                weights = w_ref[rows, qc].astype(jnp.float32)
                ds_ref[rows, qc] = (weights * (dp - delta)).astype(jnp.bfloat16)
        dq_wide = mm(kt_ref[...], ds_ref[:, wide]) * SCALE
        for n in range(WIDE):
            cols = slice((first + n) * DH, (first + n + 1) * DH)
            dq_ref[:, cols] = dq_wide[:, n * TOK : (n + 1) * TOK].T.astype(jnp.bfloat16)
    qs = jnp.concatenate([q_ref[:, h * DH : (h + 1) * DH] for h in range(GROUP)], axis=0)
    gs = jnp.concatenate([g_ref[:, h * DH : (h + 1) * DH] for h in range(GROUP)], axis=0)
    for d in range(SLOTS):
        rows = slice(d * TOK, (d + 1) * TOK)
        dkv[d][0] = (mm(ds_ref[rows], qs) * SCALE).astype(jnp.bfloat16)
        dkv[d][1] = mm(w_ref[rows], gs).astype(jnp.bfloat16)


def attend(lo, query_rows, out_grad, kvs, first, skip, heads, earlier):
    big = pl.BlockSpec((TOK, GROUP * DH), lambda i: (0, first + i))
    small = pl.BlockSpec((2, TOK, DH), lambda i: (0, 0, skip + i))
    part = pl.BlockSpec((2, TOK, DH), lambda i: (0, 0, i))
    aliased = len(earlier)
    big_shape = jax.ShapeDtypeStruct(query_rows.shape, jnp.bfloat16)
    small_shape = jax.ShapeDtypeStruct((2, TOK, heads * DH), jnp.bfloat16)
    window = SLOTS * TOK
    pairs = heads * GROUP * TOK * window
    return pl.pallas_call(
        functools.partial(attention_body, aliased),
        grid=(heads,),
        in_specs=[pl.BlockSpec((1, TOK), lambda i: (0, 0)), big, big]
        + [small] * SLOTS
        + [pl.BlockSpec(memory_space=pl.ANY)] * aliased,
        out_specs=[big, big] + [part] * SLOTS,
        out_shape=[big_shape, big_shape] + [small_shape] * SLOTS,
        scratch_shapes=[
            pltpu.VMEM((window, TOK), jnp.float32),
            pltpu.VMEM((2, window, TOK), jnp.float32),
            pltpu.VMEM((window, GROUP * TOK), jnp.bfloat16),
            pltpu.VMEM((window, GROUP * TOK), jnp.bfloat16),
            pltpu.VMEM((DH, window), jnp.bfloat16),
            pltpu.VMEM((DH, window), jnp.bfloat16),
            pltpu.VMEM((DH, GROUP * TOK), jnp.bfloat16),
            pltpu.VMEM((DH, GROUP * TOK), jnp.bfloat16),
        ],
        input_output_aliases={3 + SLOTS + n: n for n in range(aliased)},
        cost_estimate=pl.CostEstimate(
            flops=24 * pairs * DH,
            bytes_accessed=heads * TOK * DH * 2 * (4 * GROUP + 4 * SLOTS),
            transcendentals=pairs,
        ),
        compiler_params=pltpu.CompilerParams(vmem_limit_bytes=48 * 2**20),
    )(lo, query_rows, out_grad, *kvs, *earlier)


def moved(value, steps, count):
    return lax.ppermute(
        value, AXES, [(i, i + steps) for i in range(count) if 0 <= i + steps < count]
    )


def swapped(value, count):
    return lax.ppermute(value, AXES, [(i, i ^ 1) for i in range(count)])


def after(value, *earlier):
    return lax.optimization_barrier((value, *earlier))[0]


def on_device(query_rows, key_rows, value_rows, out_grad, doc_lengths):
    count = lax.axis_size(AXES)
    me = lax.axis_index(AXES)
    even = (me % 2) == 0
    ends = jnp.cumsum(doc_lengths, dtype=jnp.int32)
    position = me * TOK + jnp.arange(TOK, dtype=jnp.int32)
    starts = jnp.max(jnp.where(ends[:, None] <= position[None, :], ends[:, None], 0), axis=0)
    lo = (starts - me * TOK)[None, :]
    f32, bf16 = jnp.float32, jnp.bfloat16
    half = KVH // 2
    width = half * DH
    own0 = jnp.stack([key_rows[:, :width], value_rows[:, :width]])
    own1 = jnp.stack([key_rows[:, width:], value_rows[:, width:]])

    def call(window, chunk, skip, heads, earlier):
        got = attend(
            lo, query_rows, out_grad, window, chunk * half + skip, skip, heads, earlier
        )
        return list(got[:2]), got[2:]

    two0 = moved(own0, 2, count)
    one0 = swapped(jnp.where(even, own0, two0), count)
    four0 = moved(two0, 2, count)
    three0 = swapped(jnp.where(even, two0, four0), count)
    two1 = moved(after(own1, two0), 2, count)
    window = [own0, one0, two0, three0, four0]
    if PRE:
        three0, two1 = lax.optimization_barrier((three0, two1))
        window[3] = three0
    sendable = after(two1, three0)
    four1 = moved(sendable, 2, count)
    one1 = swapped(jnp.where(even, own1, sendable), count)
    big, a = call(window, 0, 0, SPLIT, [])
    three1 = swapped(jnp.where(even, two1, four1), count)
    if TIE:
        tied = lax.optimization_barrier((big, four1, one1))
        big, four1, one1 = tied
    big, b = call(window, 0, SPLIT, half - SPLIT, big)
    p0, p1, p2, p3, p4 = [jnp.concatenate(pair, axis=2) for pair in zip(a, b)]
    y3 = swapped(p3, count)
    window = [own1, one1, two1, three1, four1]
    big, a = call(window, 1, 0, SPLIT, big)
    if TIE:
        big, y3 = lax.optimization_barrier((big, y3))
    y1 = swapped(after(p1, y3), count).astype(f32)
    y3 = y3.astype(f32)
    s4 = (p4.astype(f32) + jnp.where(even, 0.0, y3)).astype(bf16)
    z4 = moved(s4, -2, count).astype(f32)
    big, b = call(window, 1, SPLIT, half - SPLIT, big)
    s2 = (p2.astype(f32) + jnp.where(even, y3, y1) + z4).astype(bf16)
    q0, q1, q2, q3, q4 = [jnp.concatenate(pair, axis=2) for pair in zip(a, b)]
    x3 = swapped(q3, count)
    z2 = moved(after(s2, big[0]), -2, count).astype(f32)
    total0 = p0.astype(f32) + jnp.where(even, y1, 0.0) + z2
    x1 = swapped(after(q1, x3), count).astype(f32)
    x3 = x3.astype(f32)
    s4 = (q4.astype(f32) + jnp.where(even, 0.0, x3)).astype(bf16)
    z4 = moved(s4, -2, count).astype(f32)
    s2 = (q2.astype(f32) + jnp.where(even, x3, x1) + z4).astype(bf16)
    z2 = moved(s2, -2, count).astype(f32)
    total1 = q0.astype(f32) + jnp.where(even, x1, 0.0) + z2
    grads = jnp.concatenate([total0.astype(bf16), total1.astype(bf16)], axis=2)
    return (big[0], big[1], grads[0], grads[1])


def solution(mesh):
    rows = P(AXES, None)
    return jax.shard_map(
        on_device,
        mesh=mesh,
        in_specs=(rows, rows, rows, rows, P()),
        out_specs=(rows, rows, rows, rows),
        check_vma=False,
    )
```
